512 devices in a mesh: ctx: 64 (over z, y), head: 2 (over core), dp: 4 (over x).
Axes of the slice: x: 4, y: 8, z: 8, core: 2. Of those that a mesh axis runs over, the one named last changes fastest.
Arguments:
- query: bfloat16 [65536, 2048], P(('dp', 'ctx'), 'head'), parts along dimension 0, may hold values from -6 to 6
- keys: bfloat16 [65536, 512], P(('dp', 'ctx'), 'head'), parts along dimension 0, may hold values from -6 to 6
- values: bfloat16 [65536, 512], P(('dp', 'ctx'), 'head'), parts along dimension 0, may hold values from -6 to 6
- output: bfloat16 [65536, 2048], P(('dp', 'ctx'), 'head'), parts along dimension 0, may hold values from -1.5 to 1.5
- output_gradient: bfloat16 [65536, 2048], P(('dp', 'ctx'), 'head'), parts along dimension 0, may hold values from -48 to 48
- row_log_norm: float32 [16, 65536], P('head', ('dp', 'ctx')), parts along dimension 1, may hold values from 4 to 7
- doc_lengths: int32 [64], P('dp'), parts along dimension 0, may hold values from 1 to 2048, as said below
Outputs:
- grad_query: bfloat16 [65536, 2048], P(('dp', 'ctx'), 'head'), parts along dimension 0
- key_gradient: bfloat16 [65536, 512], P(('dp', 'ctx'), 'head'), parts along dimension 0
- value_gradient: bfloat16 [65536, 512], P(('dp', 'ctx'), 'head'), parts along dimension 0
The draws below stay inside these ranges and needn't reach their ends.
There are 4 independent parts, one for each index of `dp`. The reference program is written for one: setup_inputs(seed, part) draws one part's arguments, and reference() takes and returns one part's arrays. A program takes and returns all parts, laid end to end along the dimension named above; each array names one. Nothing has to cross between parts.
Inputs may be any that keep to these rules, and one draw needn't show every extreme that they name: `doc_lengths`: the 16 documents fill the 16384 positions in order; one of them, at any place, holds exactly 2048 tokens.
All inputs are finite; a program needn't handle non-finite values.
Results may differ from the reference program's by a relative error of at most 0.013.
Values may be sent and summed in bfloat16 or wider, within the bound.
No kernel may reach another device: no remote copies, remote signals or barrier semaphores. Data moves between devices by JAX's collectives and lax.ppermute only.
A program may use at most 128 MiB of HBM per device.

```python
import math
import jax
import jax.numpy as jnp
from jax import lax

HEAD_WIDTH = 128
QUERY_HEADS = 16
KEY_VALUE_HEADS = 4
MOST = 2048
ROW_TOKENS = 16384
NDOCS = 16


def draw_doc_lengths(key, part):
    key = jax.random.fold_in(key, 11)
    cut_key = jax.random.fold_in(key, 1)
    place_key = jax.random.fold_in(key, 2)
    others = NDOCS - 1
    remain = ROW_TOKENS - MOST
    if remain - others + 1 <= MOST:
        order = jax.random.permutation(cut_key, remain - 1).astype(jnp.int32) + 1
        cuts = jnp.sort(order[:others - 1]).astype(jnp.int32)
        bounds = jnp.concatenate([jnp.zeros((1,), jnp.int32), cuts, jnp.full((1,), remain, jnp.int32)])
        lengths_rest = (bounds[1:] - bounds[:-1]).astype(jnp.int32)
    else:
        base_len = remain // others
        extra = remain - base_len * others
        reach = (base_len - 1) // 2
        shifts = jax.random.randint(cut_key, (others - 1,), -reach, reach + 1).astype(jnp.int32)
        zero_one = jnp.zeros((1,), jnp.int32)
        after = jnp.concatenate([shifts, zero_one])
        before = jnp.concatenate([zero_one, shifts])
        lengths_rest = base_len + after - before
        lengths_rest = lengths_rest.at[others - 1].add(extra)
    place = jax.random.randint(place_key, (), 0, NDOCS).astype(jnp.int32)
    slots = jnp.arange(NDOCS, dtype=jnp.int32)
    source = jnp.clip(jnp.where(slots < place, slots, slots - 1), 0, others - 1).astype(jnp.int32)
    picked = jnp.take(lengths_rest, source)
    return jnp.where(slots == place, MOST, picked).astype(jnp.int32)


def levels(stream_key, dims, shards, smallest, largest):
    gain, own = 1.0, jax.random.fold_in(stream_key, 6)
    for axis_at, shards_of in shards:
        steps = jnp.exp(jax.random.uniform(jax.random.fold_in(own, axis_at), (shards_of,), jnp.float32, smallest / len(shards), largest / len(shards)))
        gain = gain * jnp.repeat(steps, dims[axis_at] // shards_of).reshape([-1 if axis == axis_at else 1 for axis in range(len(dims))])
    return gain


def scatter_about(stream_key, dims, scale, bound, split=(), kind=jnp.bfloat16):
    values = scale * jax.random.normal(stream_key, dims, jnp.float32)
    if split:
        values = values * levels(stream_key, dims, split, -0.22, 0.18)
    return jnp.clip(values, -bound, bound).astype(kind)


def setup_inputs(seed: int = 0, part: int = 0) -> dict:
    key_of = jax.random.split(jax.random.key(seed), 8)
    own_keys = jax.random.split(jax.random.fold_in(key_of[7], part), 8)
    return {
        "query": scatter_about(own_keys[0], (ROW_TOKENS, QUERY_HEADS * HEAD_WIDTH), 1.0, 6.0, ((0, 64), (1, 2))),
        "keys": scatter_about(own_keys[1], (ROW_TOKENS, KEY_VALUE_HEADS * HEAD_WIDTH), 1.0, 6.0, ((0, 64), (1, 2))),
        "values": scatter_about(own_keys[2], (ROW_TOKENS, KEY_VALUE_HEADS * HEAD_WIDTH), 1.0, 6.0, ((0, 64), (1, 2))),
        "output": scatter_about(own_keys[3], (ROW_TOKENS, QUERY_HEADS * HEAD_WIDTH), 0.1, 1.5, ((0, 64), (1, 2))),
        "output_gradient": scatter_about(own_keys[4], (ROW_TOKENS, QUERY_HEADS * HEAD_WIDTH), 8.0, 48.0, ((0, 64), (1, 2))),
        "row_log_norm": jnp.clip(4.0 + 3.0 * jax.random.uniform(own_keys[5], (QUERY_HEADS, ROW_TOKENS), jnp.float32) ** levels(own_keys[5], (QUERY_HEADS, ROW_TOKENS), ((0, 2), (1, 64)), -0.2, 0.2), 4.0, 7.0),
        "doc_lengths": draw_doc_lengths(jax.random.fold_in(jax.random.fold_in(key_of[7], part), 71), part),
    }


def locate_docs(positions, doc_ends):
    return jnp.sum((doc_ends[None, :] <= positions[:, None]).astype(jnp.int32), axis=1)


def reference(query, keys, values, output, output_gradient, row_log_norm, doc_lengths):
    query_group_size = QUERY_HEADS // KEY_VALUE_HEADS
    softmax_scale = HEAD_WIDTH ** -0.5
    query_gathered = query.astype(jnp.float32).reshape(ROW_TOKENS, KEY_VALUE_HEADS, query_group_size, HEAD_WIDTH)
    output_gradient_gathered = output_gradient.astype(jnp.float32).reshape(ROW_TOKENS, KEY_VALUE_HEADS, query_group_size, HEAD_WIDTH)
    output_gathered = output.astype(jnp.float32).reshape(ROW_TOKENS, KEY_VALUE_HEADS, query_group_size, HEAD_WIDTH)
    key_gathered = keys.astype(jnp.float32).reshape(ROW_TOKENS, KEY_VALUE_HEADS, HEAD_WIDTH)
    value_gathered = values.astype(jnp.float32).reshape(ROW_TOKENS, KEY_VALUE_HEADS, HEAD_WIDTH)
    log_norm_gathered = row_log_norm.astype(jnp.float32).reshape(KEY_VALUE_HEADS, query_group_size, ROW_TOKENS)
    delta_gathered = jnp.einsum("wokc,wokc->okw", output_gradient_gathered, output_gathered)
    doc_ends = jnp.cumsum(doc_lengths).astype(jnp.int32)
    block = math.gcd(ROW_TOKENS, 512)
    count = ROW_TOKENS // block
    width = min(ROW_TOKENS, MOST + block)

    def one_block(carry, index):
        key_gradient_gathered, value_gradient_gathered = carry
        qstart = (index * block).astype(jnp.int32)
        kstart = jnp.maximum(qstart + block - width, 0).astype(jnp.int32)
        qpos = qstart + jnp.arange(block, dtype=jnp.int32)
        kpos = kstart + jnp.arange(width, dtype=jnp.int32)
        live = (locate_docs(qpos, doc_ends)[:, None] == locate_docs(kpos, doc_ends)[None, :]) & (kpos[None, :] <= qpos[:, None])
        query_block = lax.dynamic_slice_in_dim(query_gathered, qstart, block, 0)
        output_gradient_block = lax.dynamic_slice_in_dim(output_gradient_gathered, qstart, block, 0)
        key_block = lax.dynamic_slice_in_dim(key_gathered, kstart, width, 0)
        value_block = lax.dynamic_slice_in_dim(value_gathered, kstart, width, 0)
        lse = lax.dynamic_slice_in_dim(log_norm_gathered, qstart, block, 2)
        delta_rows = lax.dynamic_slice_in_dim(delta_gathered, qstart, block, 2)
        score_matrix = jnp.einsum("wmax,pmx->mawp", query_block, key_block) * softmax_scale
        prob = jnp.where(live[None, None], jnp.exp(score_matrix - lse[..., None]), 0.0)
        probability_block = lax.optimization_barrier(prob.astype(jnp.bfloat16)).astype(jnp.float32)
        probability_gradient = jnp.einsum("wmax,pmx->mawp", output_gradient_block, value_block)
        score_gradient = lax.optimization_barrier((prob * (probability_gradient - delta_rows[..., None])).astype(jnp.bfloat16)).astype(jnp.float32)
        value_gradient_piece = jnp.einsum("vfiy,ivfq->yvq", probability_block, output_gradient_block)
        key_gradient_piece = jnp.einsum("vfiy,ivfq->yvq", score_gradient, query_block)
        query_gradient_piece = jnp.einsum("vyxz,zvh->xvyh", score_gradient, key_block)
        key_gradient_gathered = lax.dynamic_update_slice_in_dim(key_gradient_gathered, lax.dynamic_slice_in_dim(key_gradient_gathered, kstart, width, 0) + key_gradient_piece, kstart, 0)
        value_gradient_gathered = lax.dynamic_update_slice_in_dim(value_gradient_gathered, lax.dynamic_slice_in_dim(value_gradient_gathered, kstart, width, 0) + value_gradient_piece, kstart, 0)
        return (key_gradient_gathered, value_gradient_gathered), query_gradient_piece

    row_start = (jnp.zeros((ROW_TOKENS, KEY_VALUE_HEADS, HEAD_WIDTH), jnp.float32), jnp.zeros((ROW_TOKENS, KEY_VALUE_HEADS, HEAD_WIDTH), jnp.float32))
    (key_gradient_gathered, value_gradient_gathered), dq_blocks = lax.scan(one_block, row_start, jnp.arange(count, dtype=jnp.int32))
    grad_query = (softmax_scale * dq_blocks.reshape(ROW_TOKENS, QUERY_HEADS * HEAD_WIDTH)).astype(jnp.bfloat16)
    key_gradient = (softmax_scale * key_gradient_gathered.reshape(ROW_TOKENS, KEY_VALUE_HEADS * HEAD_WIDTH)).astype(jnp.bfloat16)
    value_gradient = value_gradient_gathered.reshape(ROW_TOKENS, KEY_VALUE_HEADS * HEAD_WIDTH).astype(jnp.bfloat16)
    return (grad_query, key_gradient, value_gradient)
```

```python
import functools
import math

import jax
import jax.numpy as jnp
from jax import lax
from jax.experimental import pallas as pl
from jax.experimental.pallas import tpu as pltpu
from jax.sharding import PartitionSpec as P

HEAD_WIDTH = 128
LOG2_E = math.log2(math.e)


def moved(array, by):
    count = lax.axis_size("ctx")
    return lax.ppermute(array, "ctx", [(i, (i + by) % count) for i in range(count)])


def doc_starts(index_ref, lengths_ref, rows):
    first = index_ref[0] * rows
    places = first + lax.broadcasted_iota(jnp.int32, (1, rows), 1)
    start = jnp.zeros((1, rows), jnp.int32)
    end = jnp.int32(0)
    for doc in range(lengths_ref.shape[0]):
        end = end + lengths_ref[doc]
        start = jnp.where(places >= end, end, start)
    return start - first


def transposed_dot(a, b):
    return lax.dot_general(a, b, (((1,), (1,)), ((), ())), preferred_element_type=jnp.float32)


def one_block(distance, starts, q, do, lse, delta, kv, dq, dkv):
    rows, width = q.shape[0], HEAD_WIDTH
    groups = kv.shape[1] // (2 * width)
    per_group = q.shape[1] // (groups * width)
    key = lax.broadcasted_iota(jnp.int32, (rows, rows), 0)
    live = key - distance * rows >= starts
    if distance == 0:
        live &= key <= lax.broadcasted_iota(jnp.int32, (rows, rows), 1)
    scale = LOG2_E * width**-0.5
    for group in range(groups):
        k = kv[:, pl.ds(group * width, width)]
        v = kv[:, pl.ds((groups + group) * width, width)]
        k_t = k.T
        dk = dv = None
        for head in range(group * per_group, (group + 1) * per_group):
            columns = pl.ds(head * width, width)
            q_h, do_h = q[:, columns], do[:, columns]
            score = transposed_dot(k, q_h) * scale - lse[pl.ds(head, 1), :] * LOG2_E
            prob = jnp.where(live, jnp.exp2(score), 0.0)
            dscore = prob * (transposed_dot(v, do_h) - delta[pl.ds(head, 1), :])
            prob, dscore = prob.astype(jnp.bfloat16), dscore.astype(jnp.bfloat16)
            dv_h = jnp.dot(prob, do_h, preferred_element_type=jnp.float32)
            dk_h = jnp.dot(dscore, q_h, preferred_element_type=jnp.float32)
            dk, dv = (dk_h, dv_h) if dk is None else (dk + dk_h, dv + dv_h)
            dq_h = jnp.dot(k_t, dscore, preferred_element_type=jnp.float32)
            if distance == 0:
                dq[columns, :] = dq_h
            else:
                dq[columns, :] += dq_h
        dkv[:, pl.ds(group * width, width)] = dk.astype(dkv.dtype)
        dkv[:, pl.ds((groups + group) * width, width)] = dv.astype(dkv.dtype)


def own_kernel(index, lengths, q, do, o, lse, kv, dq, dkv, delta):
    rows, heads = q.shape[0], lse.shape[0]
    lane = lax.broadcasted_iota(jnp.int32, (rows, HEAD_WIDTH), 1)
    sums = jnp.zeros((rows, HEAD_WIDTH), jnp.float32)
    for head in range(heads):
        columns = pl.ds(head * HEAD_WIDTH, HEAD_WIDTH)
        product = do[:, columns].astype(jnp.float32) * o[:, columns].astype(jnp.float32)
        sums = jnp.where(lane == head, jnp.sum(product, axis=1, keepdims=True), sums)
    delta[...] = sums.T[:heads]
    one_block(0, doc_starts(index, lengths, rows), q, do, lse, delta, kv, dq, dkv)


def pair_kernel(distances, index, lengths, q, do, lse, delta, kv_a, kv_b, dq_in, dq, dkv_a, dkv_b):
    starts = doc_starts(index, lengths, q.shape[0])
    dq[...] = dq_in[...]
    for distance, kv, dkv in zip(distances, (kv_a, kv_b), (dkv_a, dkv_b)):
        one_block(distance, starts, q, do, lse, delta, kv, dq, dkv)


def turn_kernel(dq_t, dq):
    for head in range(dq.shape[1] // HEAD_WIDTH):
        columns = pl.ds(head * HEAD_WIDTH, HEAD_WIDTH)
        dq[:, columns] = (dq_t[columns, :].T * HEAD_WIDTH**-0.5).astype(dq.dtype)


VMEM = pl.BlockSpec(memory_space=pltpu.VMEM)
SMEM = pl.BlockSpec(memory_space=pltpu.SMEM)


def call(kernel, name, scalars, arrays, outs, blocks, rows, heads):
    return pl.pallas_call(
        kernel,
        name=name,
        out_shape=outs,
        in_specs=[SMEM] * scalars + [VMEM] * (arrays - scalars),
        out_specs=[VMEM] * len(outs),
        cost_estimate=pl.CostEstimate(
            flops=2 * 10 * blocks * heads * rows * rows * HEAD_WIDTH,
            bytes_accessed=4 << 20,
            transcendentals=blocks * heads * rows * rows,
        ),
        compiler_params=pltpu.CompilerParams(vmem_limit_bytes=32 << 20),
    )


def body(query, keys, values, output, output_gradient, row_log_norm, doc_lengths):
    rows, heads = query.shape[0], row_log_norm.shape[0]
    scale = HEAD_WIDTH**-0.5
    index = lax.axis_index("ctx").astype(jnp.int32).reshape(1)
    kv = jnp.concatenate([keys, values], axis=1)
    dq_shape = jax.ShapeDtypeStruct((query.shape[1], rows), jnp.float32)
    part_shape = jax.ShapeDtypeStruct(kv.shape, jnp.bfloat16)

    up, down = [kv], [moved(kv, 8)]
    for _ in range(4):
        up.append(moved(up[-1], 1))
    for _ in range(3):
        down.append(moved(down[-1], -1))

    dq, own, delta = call(
        own_kernel,
        "own_block",
        2,
        7,
        [
            dq_shape,
            jax.ShapeDtypeStruct(kv.shape, jnp.float32),
            jax.ShapeDtypeStruct((heads, rows), jnp.float32),
        ],
        1,
        rows,
        heads,
    )(index, doc_lengths, query, output_gradient, output, row_log_norm, kv)
    parts = {}
    for near in range(1, 5):
        far = 9 - near
        dq, parts[near], parts[far] = call(
            functools.partial(pair_kernel, (near, far)),
            f"blocks_{near}_{far}",
            2,
            9,
            [dq_shape, part_shape, part_shape],
            2,
            rows,
            heads,
        )(
            index,
            doc_lengths,
            query,
            output_gradient,
            row_log_norm,
            delta,
            up[near],
            down[near - 1],
            dq,
        )

    def joined(a, b):
        return (a.astype(jnp.float32) + b.astype(jnp.float32)).astype(jnp.bfloat16)

    near, far = parts[4], parts[5]
    for step in range(1, 4):
        near = joined(moved(near, -1), parts[4 - step])
        far = joined(moved(far, 1), parts[5 + step])
    near, far = moved(near, -1), moved(far, -8)
    total = own + near.astype(jnp.float32) + far.astype(jnp.float32)

    (grad_query,) = call(
        turn_kernel,
        "turn_query_gradient",
        0,
        1,
        [jax.ShapeDtypeStruct(query.shape, jnp.bfloat16)],
        0,
        rows,
        heads,
    )(dq)
    split = keys.shape[1]
    key_gradient = (scale * total[:, :split]).astype(jnp.bfloat16)
    value_gradient = total[:, split:].astype(jnp.bfloat16)
    return grad_query, key_gradient, value_gradient


def solution(mesh):
    tokens = P(("dp", "ctx"), "head")
    return jax.shard_map(
        body,
        mesh=mesh,
        in_specs=(tokens,) * 5 + (P("head", ("dp", "ctx")), P("dp")),
        out_specs=(tokens,) * 3,
        check_vma=False,
    )
```

```python
import functools
import math

import jax
import jax.numpy as jnp
from jax import lax
from jax.experimental import pallas as pl
from jax.experimental.pallas import tpu as pltpu
from jax.sharding import PartitionSpec as P

HEAD_WIDTH = 128
LOG2_E = math.log2(math.e)


def moved(array, by):
    count = lax.axis_size("ctx")
    return lax.ppermute(array, "ctx", [(i, (i + by) % count) for i in range(count)])


def doc_starts(index_ref, lengths_ref, rows):
    first = index_ref[0] * rows
    places = first + lax.broadcasted_iota(jnp.int32, (1, rows), 1)
    start = jnp.zeros((1, rows), jnp.int32)
    end = jnp.int32(0)
    for doc in range(lengths_ref.shape[0]):
        end = end + lengths_ref[doc]
        start = jnp.where(places >= end, end, start)
    return start - first


def transposed_dot(a, b):
    return lax.dot_general(a, b, (((1,), (1,)), ((), ())), preferred_element_type=jnp.float32)


def one_block(distance, starts, q, do, lse, delta, kv, dq, dkv):
    rows, width = q.shape[0], HEAD_WIDTH
    groups = kv.shape[1] // (2 * width)
    per_group = q.shape[1] // (groups * width)
    key = lax.broadcasted_iota(jnp.int32, (rows, rows), 0)
    live = key - distance * rows >= starts
    if distance == 0:
        live &= key <= lax.broadcasted_iota(jnp.int32, (rows, rows), 1)
    scale = LOG2_E * width**-0.5

    def group_heads(group):
        return [pl.ds(h * width, width) for h in range(group * per_group, (group + 1) * per_group)]

    held = []
    for group in range(groups):
        k = kv[:, pl.ds(group * width, width)]
        v = kv[:, pl.ds((groups + group) * width, width)]
        probs, dscores = [], []
        for n, columns in enumerate(group_heads(group)):
            head = pl.ds(group * per_group + n, 1)
            score = transposed_dot(k, q[:, columns]) * scale - lse[head, :] * LOG2_E
            prob = jnp.where(live, jnp.exp2(score), 0.0)
            dscore = prob * (transposed_dot(v, do[:, columns]) - delta[head, :])
            probs.append(prob.astype(jnp.bfloat16))
            dscores.append(dscore.astype(jnp.bfloat16))
        held.append((jnp.concatenate(probs, axis=1), jnp.concatenate(dscores, axis=1), k.T))
    for group, (prob, dscore, k_t) in enumerate(held):
        dq_group = jnp.dot(k_t, dscore, preferred_element_type=jnp.float32)
        for n, columns in enumerate(group_heads(group)):
            dq_head = dq_group[:, n * rows : (n + 1) * rows]
            if distance == 0:
                dq[columns, :] = dq_head
            else:
                dq[columns, :] += dq_head
        q_rows = jnp.concatenate([q[:, columns] for columns in group_heads(group)], axis=0)
        do_rows = jnp.concatenate([do[:, columns] for columns in group_heads(group)], axis=0)
        dk = jnp.dot(dscore, q_rows, preferred_element_type=jnp.float32)
        dv = jnp.dot(prob, do_rows, preferred_element_type=jnp.float32)
        dkv[:, pl.ds(group * width, width)] = dk.astype(dkv.dtype)
        dkv[:, pl.ds((groups + group) * width, width)] = dv.astype(dkv.dtype)


def join_kernel(keys, values, kv, sems):
    width = keys.shape[1]
    copies = [
        pltpu.make_async_copy(keys, kv.at[:, pl.ds(0, width)], sems.at[0]),
        pltpu.make_async_copy(values, kv.at[:, pl.ds(width, width)], sems.at[1]),
    ]
    for copy in copies:
        copy.start()
    for copy in copies:
        copy.wait()


def own_kernel(index, lengths, q, do, o, lse, kv, dq, dkv, delta, starts):
    rows, heads = q.shape[0], lse.shape[0]
    lane = lax.broadcasted_iota(jnp.int32, (rows, HEAD_WIDTH), 1)
    sums = jnp.zeros((rows, HEAD_WIDTH), jnp.float32)
    for head in range(heads):
        columns = pl.ds(head * HEAD_WIDTH, HEAD_WIDTH)
        product = do[:, columns].astype(jnp.float32) * o[:, columns].astype(jnp.float32)
        sums = jnp.where(lane == head, jnp.sum(product, axis=1, keepdims=True), sums)
    delta[...] = sums.T[:heads]
    starts[...] = doc_starts(index, lengths, rows)
    one_block(0, starts[...], q, do, lse, delta, kv, dq, dkv)


def block_kernel(distance, starts, q, do, lse, delta, kv, dq_in, dq, dkv):
    del dq_in
    one_block(distance, starts[...], q, do, lse, delta, kv, dq, dkv)


def turn_kernel(dq_t, dq):
    for head in range(dq.shape[1] // HEAD_WIDTH):
        columns = pl.ds(head * HEAD_WIDTH, HEAD_WIDTH)
        dq[:, columns] = (dq_t[columns, :].T * HEAD_WIDTH**-0.5).astype(dq.dtype)


def total_kernel(own, *refs):
    *parts, key_gradient, value_gradient = refs
    split = key_gradient.shape[1]
    total = own[...]
    for part in parts:
        total += part[...].astype(jnp.float32)
    key_gradient[...] = (total[:, :split] * HEAD_WIDTH**-0.5).astype(key_gradient.dtype)
    value_gradient[...] = total[:, split:].astype(value_gradient.dtype)


VMEM = pl.BlockSpec(memory_space=pltpu.VMEM)
SMEM = pl.BlockSpec(memory_space=pltpu.SMEM)


def call(kernel, name, scalars, arrays, outs, flops, aliases=None):
    return pl.pallas_call(
        kernel,
        name=name,
        out_shape=outs,
        in_specs=[SMEM] * scalars + [VMEM] * arrays,
        out_specs=[VMEM] * len(outs),
        input_output_aliases=aliases or {},
        cost_estimate=pl.CostEstimate(flops=flops, bytes_accessed=3 << 20, transcendentals=flops // 1280),
        compiler_params=pltpu.CompilerParams(vmem_limit_bytes=32 << 20),
    )


def body(query, keys, values, output, output_gradient, row_log_norm, doc_lengths):
    rows, heads = query.shape[0], row_log_norm.shape[0]
    bf16, f32 = jnp.bfloat16, jnp.float32
    index = lax.axis_index("ctx").astype(jnp.int32).reshape(1)
    joined_shape = (rows, 2 * keys.shape[1])
    dq_shape = jax.ShapeDtypeStruct((query.shape[1], rows), f32)
    flops = 10 * heads * rows * rows * HEAD_WIDTH
    own_outs = [
        dq_shape,
        jax.ShapeDtypeStruct(joined_shape, f32),
        jax.ShapeDtypeStruct((heads, rows), f32),
        jax.ShapeDtypeStruct((1, rows), jnp.int32),
    ]

    kv = pl.pallas_call(
        join_kernel,
        name="keys_and_values",
        out_shape=jax.ShapeDtypeStruct(joined_shape, bf16),
        in_specs=[pl.BlockSpec(memory_space=pltpu.HBM)] * 2,
        out_specs=VMEM,
        scratch_shapes=[pltpu.SemaphoreType.DMA((2,))],
        cost_estimate=pl.CostEstimate(flops=0, bytes_accessed=1 << 19, transcendentals=0),
    )(keys, values)
    dq, own, delta, starts = call(own_kernel, "own_block", 2, 5, own_outs, flops)(
        index, doc_lengths, query, output_gradient, output, row_log_norm, kv
    )

    def block(distance, kv, dq):
        outs = [dq_shape, jax.ShapeDtypeStruct(joined_shape, bf16)]
        kernel = functools.partial(block_kernel, distance)
        return call(kernel, f"block_{distance}", 0, 7, outs, flops, {6: 0})(
            starts, query, output_gradient, row_log_norm, delta, kv, dq
        )

    def joined(*parts):
        return sum(part.astype(f32) for part in parts).astype(bf16)

    tie = lax.optimization_barrier
    got, part = {}, {}
    got[1], got[8] = moved(kv, 1), moved(kv, 8)
    for near in range(1, 4):
        far = 9 - near
        got[near], dq = tie((got[near], dq))
        got[near + 1] = moved(got[near], 1)
        dq, part[near] = block(near, got[near], dq)
        got[far], dq = tie((got[far], dq))
        got[far - 1] = moved(got[far], -1)
        dq, part[far] = block(far, got[far], dq)

    dq, part[4] = block(4, got[4], dq)
    near = moved(part[4], -1)
    dq, part[5] = block(5, got[5], dq)
    far = moved(part[5], 1)
    home = [moved(part[8], -8)]
    near = moved(joined(near, part[3]), -1)
    far = moved(joined(far, part[6]), 1)
    near = moved(joined(near, part[2]), -1)
    far = moved(joined(far, part[7]), -7)
    near = moved(joined(near, part[1]), -1)
    home += [near, far]
    (grad_query,) = call(turn_kernel, "turn_query_gradient", 0, 1, [jax.ShapeDtypeStruct(query.shape, bf16)], 0)(dq)
    half = jax.ShapeDtypeStruct(keys.shape, bf16)
    key_gradient, value_gradient = call(total_kernel, "total", 0, 1 + len(home), [half, half], 0)(own, *home)
    return grad_query, key_gradient, value_gradient


def solution(mesh):
    tokens = P(("dp", "ctx"), "head")
    return jax.shard_map(
        body,
        mesh=mesh,
        in_specs=(tokens,) * 5 + (P("head", ("dp", "ctx")), P("dp")),
        out_specs=(tokens,) * 3,
        check_vma=False,
    )
```

```python
import functools
import math

import jax
import jax.numpy as jnp
from jax import lax
from jax.experimental import pallas as pl
from jax.experimental.pallas import tpu as pltpu
from jax.sharding import PartitionSpec as P

HEAD_WIDTH = 128
LOG2_E = math.log2(math.e)


def moved(array, by):
    count = lax.axis_size("ctx")
    return lax.ppermute(array, "ctx", [(i, i + by) for i in range(max(0, -by), min(count, count - by))])


def turned(array, by):
    count = lax.axis_size("ctx")
    return lax.ppermute(array, "ctx", [(i, (i + by) % count) for i in range(count)])


def doc_starts(index_ref, lengths_ref, rows):
    first = index_ref[0] * rows
    places = first + lax.broadcasted_iota(jnp.int32, (1, rows), 1)
    start = jnp.zeros((1, rows), jnp.int32)
    end = jnp.int32(0)
    for doc in range(lengths_ref.shape[0]):
        end = end + lengths_ref[doc]
        start = jnp.where(places >= end, end, start)
    return start - first


def transposed_dot(a, b):
    return lax.dot_general(a, b, (((1,), (1,)), ((), ())), preferred_element_type=jnp.float32)


def one_block(distance, starts, q, do, lse, delta, kv, dq_before, dq, dkv):
    rows, width = q.shape[0], HEAD_WIDTH
    groups = kv.shape[1] // (2 * width)
    per_group = q.shape[1] // (groups * width)
    key = lax.broadcasted_iota(jnp.int32, (rows, rows), 0)
    live = key - distance * rows >= starts
    if distance == 0:
        live &= key <= lax.broadcasted_iota(jnp.int32, (rows, rows), 1)
    scale = LOG2_E * width**-0.5

    def group_heads(group):
        return [pl.ds(h * width, width) for h in range(group * per_group, (group + 1) * per_group)]

    held = []
    for group in range(groups):
        k = kv[:, pl.ds(group * width, width)]
        v = kv[:, pl.ds((groups + group) * width, width)]
        probs, dscores = [], []
        for n, columns in enumerate(group_heads(group)):
            head = pl.ds(group * per_group + n, 1)
            score = transposed_dot(k, q[:, columns]) * scale - lse[head, :] * LOG2_E
            prob = jnp.where(live, jnp.exp2(score), 0.0)
            dscore = prob * (transposed_dot(v, do[:, columns]) - delta[head, :])
            probs.append(prob.astype(jnp.bfloat16))
            dscores.append(dscore.astype(jnp.bfloat16))
        held.append((jnp.concatenate(probs, axis=1), jnp.concatenate(dscores, axis=1), k.T))
    for group, (prob, dscore, k_t) in enumerate(held):
        dq_group = jnp.dot(k_t, dscore, preferred_element_type=jnp.float32)
        for n, columns in enumerate(group_heads(group)):
            dq_head = dq_group[:, n * rows : (n + 1) * rows]
            dq[columns, :] = dq_head if dq_before is None else dq_before[columns, :] + dq_head
        q_rows = jnp.concatenate([q[:, columns] for columns in group_heads(group)], axis=0)
        do_rows = jnp.concatenate([do[:, columns] for columns in group_heads(group)], axis=0)
        dk = jnp.dot(dscore, q_rows, preferred_element_type=jnp.float32)
        dv = jnp.dot(prob, do_rows, preferred_element_type=jnp.float32)
        dkv[:, pl.ds(group * width, width)] = dk.astype(dkv.dtype)
        dkv[:, pl.ds((groups + group) * width, width)] = dv.astype(dkv.dtype)


def join_kernel(keys, values, kv, sems):
    width = keys.shape[1]
    copies = [
        pltpu.make_async_copy(keys, kv.at[:, pl.ds(0, width)], sems.at[0]),
        pltpu.make_async_copy(values, kv.at[:, pl.ds(width, width)], sems.at[1]),
    ]
    for copy in copies:
        copy.start()
    for copy in copies:
        copy.wait()


def own_kernel(index, lengths, q, do, o, lse, kv, dq, dkv, delta, starts):
    rows, heads = q.shape[0], lse.shape[0]
    lane = lax.broadcasted_iota(jnp.int32, (rows, HEAD_WIDTH), 1)
    sums = jnp.zeros((rows, HEAD_WIDTH), jnp.float32)
    for head in range(heads):
        columns = pl.ds(head * HEAD_WIDTH, HEAD_WIDTH)
        product = do[:, columns].astype(jnp.float32) * o[:, columns].astype(jnp.float32)
        sums = jnp.where(lane == head, jnp.sum(product, axis=1, keepdims=True), sums)
    delta[...] = sums.T[:heads]
    starts[...] = doc_starts(index, lengths, rows)
    one_block(0, starts[...], q, do, lse, delta, kv, None, dq, dkv)


def block_kernel(distance, starts, q, do, lse, delta, kv, dq_before, dq, dkv):
    reached = jnp.min(starts[...]) < -(distance - 1) * q.shape[0]

    @pl.when(reached)
    def _():
        one_block(distance, starts[...], q, do, lse, delta, kv, dq_before, dq, dkv)

    @pl.when(jnp.logical_not(reached))
    def _():
        dq[...] = dq_before[...]
        dkv[...] = jnp.zeros_like(dkv)


def turn_kernel(dq_t, dq):
    for head in range(dq.shape[1] // HEAD_WIDTH):
        columns = pl.ds(head * HEAD_WIDTH, HEAD_WIDTH)
        dq[:, columns] = (dq_t[columns, :].T * HEAD_WIDTH**-0.5).astype(dq.dtype)


def total_kernel(own, *refs):
    *parts, key_gradient, value_gradient = refs
    split = key_gradient.shape[1]
    total = own[...]
    for part in parts:
        total += part[...].astype(jnp.float32)
    key_gradient[...] = (total[:, :split] * HEAD_WIDTH**-0.5).astype(key_gradient.dtype)
    value_gradient[...] = total[:, split:].astype(value_gradient.dtype)


VMEM = pl.BlockSpec(memory_space=pltpu.VMEM)
SMEM = pl.BlockSpec(memory_space=pltpu.SMEM)


def call(kernel, name, scalars, arrays, outs, flops, aliases=None):
    return pl.pallas_call(
        kernel,
        name=name,
        out_shape=outs,
        in_specs=[SMEM] * scalars + [VMEM] * arrays,
        out_specs=[VMEM] * len(outs),
        input_output_aliases=aliases or {},
        cost_estimate=pl.CostEstimate(flops=flops, bytes_accessed=3 << 20, transcendentals=flops // 1280),
        compiler_params=pltpu.CompilerParams(vmem_limit_bytes=32 << 20),
    )


def body(query, keys, values, output, output_gradient, row_log_norm, doc_lengths):
    rows, heads = query.shape[0], row_log_norm.shape[0]
    bf16, f32 = jnp.bfloat16, jnp.float32
    index = lax.axis_index("ctx").astype(jnp.int32).reshape(1)
    joined_shape = (rows, 2 * keys.shape[1])
    dq_shape = jax.ShapeDtypeStruct((query.shape[1], rows), f32)
    flops = 10 * heads * rows * rows * HEAD_WIDTH
    own_outs = [
        dq_shape,
        jax.ShapeDtypeStruct(joined_shape, f32),
        jax.ShapeDtypeStruct((heads, rows), f32),
        jax.ShapeDtypeStruct((1, rows), jnp.int32),
    ]

    kv = pl.pallas_call(
        join_kernel,
        name="keys_and_values",
        out_shape=jax.ShapeDtypeStruct(joined_shape, bf16),
        in_specs=[pl.BlockSpec(memory_space=pltpu.HBM)] * 2,
        out_specs=VMEM,
        scratch_shapes=[pltpu.SemaphoreType.DMA((2,))],
        cost_estimate=pl.CostEstimate(flops=0, bytes_accessed=1 << 19, transcendentals=0),
    )(keys, values)
    dq, own, delta, starts = call(own_kernel, "own_block", 2, 5, own_outs, flops)(
        index, doc_lengths, query, output_gradient, output, row_log_norm, kv
    )

    def block(distance, kv, dq):
        outs = [dq_shape, jax.ShapeDtypeStruct(joined_shape, bf16)]
        kernel = functools.partial(block_kernel, distance)
        return call(kernel, f"block_{distance}", 0, 7, outs, flops, {6: 0})(
            starts, query, output_gradient, row_log_norm, delta, kv, dq
        )

    def joined(*parts):
        return sum(part.astype(f32) for part in parts).astype(bf16)

    tie = lax.optimization_barrier
    got, part = {}, {}
    got[1], got[8] = moved(kv, 1), turned(kv, 8)
    for near in range(1, 4):
        far = 9 - near
        got[near], dq = tie((got[near], dq))
        got[near + 1] = moved(got[near], 1)
        dq, part[near] = block(near, got[near], dq)
        got[far], dq = tie((got[far], dq))
        got[far - 1] = turned(got[far], -1)
        if near < 3:
            dq, part[far] = block(far, got[far], dq)

    dq, part[4] = block(4, got[4], dq)
    near = moved(part[4], -1)
    dq, part[5] = block(5, got[5], dq)
    dq, part[6] = block(6, got[6], dq)
    far, far_by = turned(part[5], 2), turned(part[6], 1)
    near = moved(joined(near, part[3]), -2)
    near_by = moved(part[2], -1)
    far = turned(joined(far, far_by, part[7]), -7)
    home = [far, moved(part[8], -8)]
    near = moved(joined(near, near_by, part[1]), -1)
    home += [near]
    (grad_query,) = call(turn_kernel, "turn_query_gradient", 0, 1, [jax.ShapeDtypeStruct(query.shape, bf16)], 0)(dq)
    half = jax.ShapeDtypeStruct(keys.shape, bf16)
    key_gradient, value_gradient = call(total_kernel, "total", 0, 1 + len(home), [half, half], 0)(own, *home)
    return grad_query, key_gradient, value_gradient


def solution(mesh):
    tokens = P(("dp", "ctx"), "head")
    return jax.shard_map(
        body,
        mesh=mesh,
        in_specs=(tokens,) * 5 + (P("head", ("dp", "ctx")), P("dp")),
        out_specs=(tokens,) * 3,
        check_vma=False,
    )
```

```python
import functools
import math

import jax
import jax.numpy as jnp
from jax import lax
from jax.experimental import pallas as pl
from jax.experimental.pallas import tpu as pltpu
from jax.sharding import PartitionSpec as P

HEAD_WIDTH = 128
LOG2_E = math.log2(math.e)


def moved(array, by):
    count = lax.axis_size("ctx")
    return lax.ppermute(array, "ctx", [(i, i + by) for i in range(max(0, -by), min(count, count - by))])


def turned(array, by):
    count = lax.axis_size("ctx")
    return lax.ppermute(array, "ctx", [(i, (i + by) % count) for i in range(count)])


def doc_starts(index_ref, lengths_ref, rows):
    first = index_ref[0] * rows
    places = first + lax.broadcasted_iota(jnp.int32, (1, rows), 1)
    start = jnp.zeros((1, rows), jnp.int32)
    end = jnp.int32(0)
    for doc in range(lengths_ref.shape[0]):
        end = end + lengths_ref[doc]
        start = jnp.where(places >= end, end, start)
    return start - first


def transposed_dot(a, b):
    return lax.dot_general(a, b, (((1,), (1,)), ((), ())), preferred_element_type=jnp.float32)


def one_block(distance, starts, q, do, lse, delta, kv, dq_before, dq, dkv):
    rows, width = q.shape[0], HEAD_WIDTH
    groups = kv.shape[1] // (2 * width)
    per_group = q.shape[1] // (groups * width)
    key = lax.broadcasted_iota(jnp.int32, (rows, rows), 0)
    live = key - distance * rows >= starts
    if distance == 0:
        live &= key <= lax.broadcasted_iota(jnp.int32, (rows, rows), 1)
    scale = LOG2_E * width**-0.5

    def group_heads(group):
        return [pl.ds(h * width, width) for h in range(group * per_group, (group + 1) * per_group)]

    held = []
    for group in range(groups):
        k = kv[:, pl.ds(group * width, width)]
        v = kv[:, pl.ds((groups + group) * width, width)]
        probs, dscores = [], []
        for n, columns in enumerate(group_heads(group)):
            head = pl.ds(group * per_group + n, 1)
            score = transposed_dot(k, q[:, columns]) * scale - lse[head, :] * LOG2_E
            prob = jnp.where(live, jnp.exp2(score), 0.0)
            dscore = prob * (transposed_dot(v, do[:, columns]) - delta[head, :])
            probs.append(prob.astype(jnp.bfloat16))
            dscores.append(dscore.astype(jnp.bfloat16))
        held.append((jnp.concatenate(probs, axis=1), jnp.concatenate(dscores, axis=1), k.T))
    for group, (prob, dscore, k_t) in enumerate(held):
        dq_group = jnp.dot(k_t, dscore, preferred_element_type=jnp.float32)
        for n, columns in enumerate(group_heads(group)):
            dq_head = dq_group[:, n * rows : (n + 1) * rows]
            dq[columns, :] = dq_head if dq_before is None else dq_before[columns, :] + dq_head
        q_rows = jnp.concatenate([q[:, columns] for columns in group_heads(group)], axis=0)
        do_rows = jnp.concatenate([do[:, columns] for columns in group_heads(group)], axis=0)
        dk = jnp.dot(dscore, q_rows, preferred_element_type=jnp.float32)
        dv = jnp.dot(prob, do_rows, preferred_element_type=jnp.float32)
        dkv[:, pl.ds(group * width, width)] = dk.astype(dkv.dtype)
        dkv[:, pl.ds((groups + group) * width, width)] = dv.astype(dkv.dtype)


def join_kernel(keys, values, kv, sems):
    width = keys.shape[1]
    copies = [
        pltpu.make_async_copy(keys, kv.at[:, pl.ds(0, width)], sems.at[0]),
        pltpu.make_async_copy(values, kv.at[:, pl.ds(width, width)], sems.at[1]),
    ]
    for copy in copies:
        copy.start()
    for copy in copies:
        copy.wait()


def own_kernel(index, lengths, q, do, o, lse, kv, dq, dkv, delta, starts):
    rows, heads = q.shape[0], lse.shape[0]
    lane = lax.broadcasted_iota(jnp.int32, (rows, HEAD_WIDTH), 1)
    sums = jnp.zeros((rows, HEAD_WIDTH), jnp.float32)
    for head in range(heads):
        columns = pl.ds(head * HEAD_WIDTH, HEAD_WIDTH)
        product = do[:, columns].astype(jnp.float32) * o[:, columns].astype(jnp.float32)
        sums = jnp.where(lane == head, jnp.sum(product, axis=1, keepdims=True), sums)
    delta[...] = sums.T[:heads]
    starts[...] = doc_starts(index, lengths, rows)
    one_block(0, starts[...], q, do, lse, delta, kv, None, dq, dkv)


def block_kernel(distance, starts, q, do, lse, delta, kv, dq_before, dq, dkv):
    reached = starts[...][0, 0] < -(distance - 1) * q.shape[0]

    @pl.when(reached)
    def _():
        one_block(distance, starts[...], q, do, lse, delta, kv, dq_before, dq, dkv)

    @pl.when(jnp.logical_not(reached))
    def _():
        dq[...] = dq_before[...]
        dkv[...] = jnp.zeros_like(dkv)


def turn_kernel(dq_t, dq):
    for head in range(dq.shape[1] // HEAD_WIDTH):
        columns = pl.ds(head * HEAD_WIDTH, HEAD_WIDTH)
        dq[:, columns] = (dq_t[columns, :].T * HEAD_WIDTH**-0.5).astype(dq.dtype)


def total_kernel(own, *refs):
    *parts, key_gradient, value_gradient = refs
    split = key_gradient.shape[1]
    total = own[...]
    for part in parts:
        total += part[...].astype(jnp.float32)
    key_gradient[...] = (total[:, :split] * HEAD_WIDTH**-0.5).astype(key_gradient.dtype)
    value_gradient[...] = total[:, split:].astype(value_gradient.dtype)


VMEM = pl.BlockSpec(memory_space=pltpu.VMEM)
SMEM = pl.BlockSpec(memory_space=pltpu.SMEM)


def call(kernel, name, scalars, arrays, outs, flops, aliases=None):
    return pl.pallas_call(
        kernel,
        name=name,
        out_shape=outs,
        in_specs=[SMEM] * scalars + [VMEM] * arrays,
        out_specs=[VMEM] * len(outs),
        input_output_aliases=aliases or {},
        cost_estimate=pl.CostEstimate(flops=flops, bytes_accessed=3 << 20, transcendentals=flops // 1280),
        compiler_params=pltpu.CompilerParams(vmem_limit_bytes=32 << 20),
    )


def body(query, keys, values, output, output_gradient, row_log_norm, doc_lengths):
    rows, heads = query.shape[0], row_log_norm.shape[0]
    bf16, f32 = jnp.bfloat16, jnp.float32
    index = lax.axis_index("ctx").astype(jnp.int32).reshape(1)
    joined_shape = (rows, 2 * keys.shape[1])
    dq_shape = jax.ShapeDtypeStruct((query.shape[1], rows), f32)
    flops = 10 * heads * rows * rows * HEAD_WIDTH
    own_outs = [
        dq_shape,
        jax.ShapeDtypeStruct(joined_shape, f32),
        jax.ShapeDtypeStruct((heads, rows), f32),
        jax.ShapeDtypeStruct((1, rows), jnp.int32),
    ]

    kv = pl.pallas_call(
        join_kernel,
        name="keys_and_values",
        out_shape=jax.ShapeDtypeStruct(joined_shape, bf16),
        in_specs=[pl.BlockSpec(memory_space=pltpu.HBM)] * 2,
        out_specs=VMEM,
        scratch_shapes=[pltpu.SemaphoreType.DMA((2,))],
        cost_estimate=pl.CostEstimate(flops=0, bytes_accessed=1 << 19, transcendentals=0),
    )(keys, values)
    dq, own, delta, starts = call(own_kernel, "own_block", 2, 5, own_outs, flops)(
        index, doc_lengths, query, output_gradient, output, row_log_norm, kv
    )

    def block(distance, kv, dq):
        outs = [dq_shape, jax.ShapeDtypeStruct(joined_shape, bf16)]
        kernel = functools.partial(block_kernel, distance)
        return call(kernel, f"block_{distance}", 0, 7, outs, flops, {6: 0})(
            starts, query, output_gradient, row_log_norm, delta, kv, dq
        )

    def joined(*parts):
        return sum(part.astype(f32) for part in parts).astype(bf16)

    tie = lax.optimization_barrier
    got, part = {}, {}
    got[1], got[8] = moved(kv, 1), turned(kv, 8)
    for near in range(1, 4):
        far = 9 - near
        got[near], dq = tie((got[near], dq))
        got[near + 1] = moved(got[near], 1)
        dq, part[near] = block(near, got[near], dq)
        got[far], dq = tie((got[far], dq))
        got[far - 1] = turned(got[far], -1)
        if near < 3:
            dq, part[far] = block(far, got[far], dq)

    dq, part[4] = block(4, got[4], dq)
    near = moved(part[4], -1)
    dq, part[6] = block(6, got[6], dq)
    far_by = turned(part[6], 1)
    dq, part[5] = block(5, got[5], dq)
    far = turned(part[5], 2)
    near = moved(joined(near, part[3]), -2)
    near_by = moved(part[2], -1)
    far = turned(joined(far, far_by, part[7]), -7)
    home = [far, moved(part[8], -8)]
    near = moved(joined(near, near_by, part[1]), -1)
    home += [near]
    (grad_query,) = call(turn_kernel, "turn_query_gradient", 0, 1, [jax.ShapeDtypeStruct(query.shape, bf16)], 0)(dq)
    half = jax.ShapeDtypeStruct(keys.shape, bf16)
    key_gradient, value_gradient = call(total_kernel, "total", 0, 1 + len(home), [half, half], 0)(own, *home)
    return grad_query, key_gradient, value_gradient


def solution(mesh):
    tokens = P(("dp", "ctx"), "head")
    return jax.shard_map(
        body,
        mesh=mesh,
        in_specs=(tokens,) * 5 + (P("head", ("dp", "ctx")), P("dp")),
        out_specs=(tokens,) * 3,
        check_vma=False,
    )
```
